128 devices in a mesh: qa: 8 (over x, y_lo), qb: 16 (over y_hi, z, core).
Axes of the slice: x: 4, y: 4 (y_hi: 2, y_lo: 2; y = y_hi * 2 + y_lo), z: 4, core: 2. Of those that a mesh axis runs over, the one named last changes fastest.
Arguments:
- amplitudes: float32 [8, 16, 128, 128, 128], P('qa', 'qb'), may hold values from -6 to 6
- gates: float32 [2, 4, 128, 128], replicated, may hold values from -0.5 to 0.5
- qubit_order: int32 [2, 4, 7], replicated, may hold values from 0 to 6, each once within a row
Outputs:
- rotated: float32 [8, 16, 128, 128, 128], P('qa', 'qb')
The draws below stay inside these ranges and needn't reach their ends.
Inputs may be any that keep to these rules, and one draw needn't show every extreme that they name: Each row of qubit_order lists every number 0 to 6 exactly once.
All inputs are finite; a program needn't handle non-finite values.
Results may differ from the reference program's by a relative error of at most 0.00011.
Values sent between devices are 32-bit elements; how exact they have to be, the bound alone decides.
No kernel may reach another device: no remote copies, remote signals or barrier semaphores. Data moves between devices by JAX's collectives and lax.ppermute only.
A program may use at most 128 MiB of HBM per device.

```python
import jax
import jax.numpy as jnp
from jax import lax

GATE = 128
BITS = 7
TURN = 3
LAYERS = 2
N_QA = 8
N_QB = 16


def shard_levels(key, shape, cuts, low, top_value):
    gain = 1.0
    for dim, shards_of in cuts:
        steps = jax.random.uniform(jax.random.fold_in(jax.random.fold_in(key, 6), dim), (shards_of,), jnp.float32, low / len(cuts), top_value / len(cuts))
        gain = gain * jnp.repeat(jnp.exp(steps), shape[dim] // shards_of).reshape((-1,) + (1,) * (len(shape) - 1 - dim))
    return gain


def normal_values(key, dims, scale, most, shards=(), held_as=jnp.bfloat16):
    drawn = scale * jax.random.normal(key, dims, jnp.float32)
    if shards:
        drawn = drawn * shard_levels(key, dims, shards, -0.22, 0.18)
    return jnp.clip(drawn, -most, most).astype(held_as)


def setup_inputs(seed: int = 0) -> dict:
    arg_keys = jax.random.split(jax.random.key(seed), 4)
    return {
        "amplitudes": normal_values(arg_keys[0], (N_QA, N_QB, GATE, GATE, GATE), 1.0, 6.0, ((0, 8), (1, 16)), jnp.float32),
        "gates": normal_values(arg_keys[1], (LAYERS, 4, GATE, GATE), GATE ** -0.5, 0.5, (), jnp.float32),
        "qubit_order": jax.vmap(lambda own: jax.random.permutation(own, BITS))(jax.random.split(arg_keys[2], LAYERS * 4)).reshape((LAYERS, 4, BITS)).astype(jnp.int32),
    }


def effective(matrix, qubit_seq):
    basis_index = jnp.arange(matrix.shape[0], dtype=jnp.int32)
    mapped = jnp.zeros_like(basis_index)
    for bit_pos in range(qubit_seq.shape[0]):
        mapped = mapped + jnp.left_shift(jnp.bitwise_and(jnp.right_shift(basis_index, qubit_seq[bit_pos]), 1), bit_pos)
    return matrix[mapped][:, mapped]


def local_layer(slab_part, front_gate, middle_gate, back_gate, shift_bits):
    outer_size = 2 ** shift_bits
    inner_size = GATE // outer_size
    tiled_view = slab_part.reshape(N_QB, outer_size, inner_size, outer_size, inner_size, outer_size, inner_size)
    folded = front_gate.reshape(inner_size, outer_size, inner_size, outer_size)
    tiled_view = jnp.einsum("deaB,yAaBbCc->yAdebCc", folded, tiled_view, precision=lax.Precision.HIGHEST)
    folded = middle_gate.reshape(inner_size, outer_size, inner_size, outer_size)
    tiled_view = jnp.einsum("debC,yAaBbCc->yAaBdec", folded, tiled_view, precision=lax.Precision.HIGHEST)
    folded = back_gate.reshape(inner_size, outer_size, inner_size, outer_size)
    tiled_view = jnp.einsum("decA,yAaBbCc->yeaBbCd", folded, tiled_view, precision=lax.Precision.HIGHEST)
    return tiled_view.reshape(slab_part.shape)


def top_first(current, top_gate):
    rest_size = GATE // N_QA
    tiled_view = current.reshape(N_QA, N_QB, N_QA, rest_size, GATE, GATE)
    top_mixer = top_gate.reshape(N_QA, rest_size, N_QA, rest_size)
    blocks = []
    for head_idx in range(N_QA):
        slab_piece = tiled_view[:, :, head_idx]
        blocks.append(jnp.einsum("mnpq,pyqbc->mynbc", top_mixer, slab_piece, precision=lax.Precision.HIGHEST))
    return jnp.stack(blocks, axis=2).reshape(N_QA, N_QB, GATE, GATE, GATE)


def top_second(current, top_gate):
    rest_size = GATE // N_QB
    tiled_view = current.reshape(N_QA, N_QB, N_QB, rest_size, GATE, GATE)
    top_mixer = top_gate.reshape(N_QB, rest_size, N_QB, rest_size)
    blocks = []
    for head_idx in range(N_QB):
        slab_piece = tiled_view[:, :, head_idx]
        blocks.append(jnp.einsum("mnpq,xpqbc->xmnbc", top_mixer, slab_piece, precision=lax.Precision.HIGHEST))
    return jnp.stack(blocks, axis=2).reshape(N_QA, N_QB, GATE, GATE, GATE)


def reference(amplitudes, gates, qubit_order):
    current = amplitudes
    for layer_idx in range(LAYERS):
        merged = [effective(gates[layer_idx, slot_idx], qubit_order[layer_idx, slot_idx]) for slot_idx in range(4)]
        shift_bits = TURN * layer_idx

        def advance(slab_part):
            return local_layer(slab_part, merged[0], merged[1], merged[2], shift_bits)

        current = lax.map(advance, current)
        if layer_idx % 2 == 0:
            current = top_first(current, merged[3])
        else:
            current = top_second(current, merged[3])
    return current
```

```python
import jax
import jax.numpy as jnp
from jax import lax
from jax.experimental import pallas as pl
from jax.experimental.pallas import tpu as pltpu
from jax.sharding import PartitionSpec as P

N = 128
BF = jnp.bfloat16
F32 = jnp.float32
F0, M0, B0, T0, F1, M1, B1, T1 = range(8)


def split(value, axis):
    high = value.astype(BF)
    low = (value - high.astype(F32)).astype(BF)
    return jnp.concatenate([high, low], axis=axis)


def turn(index, low_bits):
    return ((index & (2**low_bits - 1)) << (7 - low_bits)) | (index >> low_bits)


ROWS = {F1: 4, B1: 4, B0: 3}
COLUMNS = {F1: 4, B1: 4}


def gates_kernel(order_ref, gates_ref, stacked_ref):
    along = lax.broadcasted_iota(jnp.int32, (N, N), 0)
    across = lax.broadcasted_iota(jnp.int32, (N, N), 1)

    def mapped(index, slot):
        total = jnp.zeros_like(index)
        for k in range(7):
            total = total + (((index >> order_ref[slot, k]) & 1) << k)
        return total

    for slot in range(8):
        rows = turn(along, ROWS[slot]) if slot in ROWS else along
        columns = turn(across, COLUMNS[slot]) if slot in COLUMNS else across
        pick_rows = (mapped(rows, slot) == across).astype(F32).astype(BF)
        pick_columns = (mapped(columns, slot) == along).astype(F32).astype(BF)
        picked = jnp.dot(
            pick_rows, split(gates_ref[slot], 1), preferred_element_type=F32
        ).astype(BF)
        both = jnp.concatenate([picked[:, :N], picked[:, N:]], axis=0)
        effective = jnp.dot(both, pick_columns, preferred_element_type=F32).astype(BF)
        stacked_ref[slot] = jnp.concatenate([effective, effective], axis=1)


def stack_gates(gates, qubit_order):
    return pl.pallas_call(
        gates_kernel,
        out_shape=jax.ShapeDtypeStruct((8, 2 * N, 2 * N), BF),
        in_specs=[
            pl.BlockSpec(memory_space=pltpu.SMEM),
            pl.BlockSpec(memory_space=pltpu.VMEM),
        ],
        out_specs=pl.BlockSpec(memory_space=pltpu.VMEM),
        name="stack_gates",
    )(qubit_order.reshape(8, 7), gates.reshape(8, N, N))


def left(gate, blocks):
    width = len(blocks) * N
    value = jnp.concatenate(blocks, axis=1) if len(blocks) > 1 else blocks[0]
    both = jnp.dot(gate, split(value, 0), preferred_element_type=F32)
    total = both[:N] + both[N:]
    return [total[:, k : k + N] for k in range(0, width, N)]


def left_of_transposed(gate, blocks):
    width = len(blocks) * N
    value = jnp.concatenate(blocks, axis=0)
    both = lax.dot_general(
        gate, split(value, 1), (((1,), (1,)), ((), ())), preferred_element_type=F32
    )
    total = both[:N] + both[N:]
    return [total[:, k : k + N] for k in range(0, width, N)]


GROUP = 2


def before_kernel(x_ref, gates_ref, out_ref, held):
    step = pl.program_id(0)

    @pl.when(step < 16)
    def _():
        gate = gates_ref[M0]
        for k in range(0, 8, GROUP):
            done = left(gate, [x_ref[k + j] for j in range(GROUP)])
            for j in range(GROUP):
                start = pl.multiple_of((step * 8 + k + j) * N, N)
                held[pl.ds(start, N), :] = done[j]

    @pl.when(step >= 16)
    def _():
        gate = gates_ref[F0]
        b0 = step - 16
        for k in range(0, 8, GROUP):
            done = left(
                gate,
                [held[pl.ds(b0 + (k + j) * 16, N, stride=N), :] for j in range(GROUP)],
            )
            for j in range(GROUP):
                out_ref[:, 0, k + j] = done[j].reshape(8, 16, N)


def between_kernel(x_ref, gates_ref, out_ref, turned, held):
    step = pl.program_id(0)

    @pl.when(step < 16)
    def _():
        gate = gates_ref[T0]
        for k in range(0, 8, GROUP):
            done = left(
                gate, [x_ref[:, 0, k + j].reshape(N, N) for j in range(GROUP)]
            )
            for j in range(GROUP):
                turned[:, k + j] = done[j].reshape(8, 16, N)
        gate = gates_ref[F1]
        for k in range(0, 8, GROUP):
            done = left(gate, [turned[k + j].reshape(N, N) for j in range(GROUP)])
            for j in range(GROUP):
                held[k + j, step] = done[j].reshape(8, 16, N)

    @pl.when(step >= 16)
    def _():
        gate = gates_ref[T1]
        x = step - 16
        for b1 in range(8):
            done = left(
                gate, [held[x, :, b1, k : k + 8].reshape(N, N) for k in (0, 8)]
            )
            for j, k in enumerate((0, 8)):
                out_ref[0, :, b1, k : k + 8] = done[j].reshape(16, 8, N)


def after_kernel(x_ref, gates_ref, out_ref, turned, held, ready):
    step = pl.program_id(0)

    @pl.when(step < 8)
    def _():
        gate = gates_ref[B0]
        for k in range(0, 16, GROUP):
            done = left_of_transposed(
                gate, [x_ref[0, k + j].reshape(N, N) for j in range(GROUP)]
            )
            for j in range(GROUP):
                turned[:, k + j] = done[j].reshape(16, 8, N)
        gate = gates_ref[M1]
        for k in range(0, 16, GROUP):
            done = left(gate, [turned[k + j].reshape(N, N) for j in range(GROUP)])
            for j in range(GROUP):
                start = pl.multiple_of((step * 16 + k + j) * N, N)
                held[pl.ds(start, N), :] = done[j]

    @pl.when((step >= 8) & (step < 24))
    def _():
        gate = gates_ref[B1]
        b0 = step - 8
        for k in range(0, 8, GROUP):
            done = left(
                gate,
                [held[pl.ds(b0 * 8 + k + j, N, stride=N), :] for j in range(GROUP)],
            )
            for j in range(GROUP):
                ready[:, b0, k + j] = done[j].reshape(8, 16, N)

    @pl.when(step >= 24)
    def _():
        a1 = step - 24
        for b0 in range(16):
            block = ready[a1, b0].reshape(N, N).T
            for b1 in range(8):
                out_ref[pl.ds(b1 * 16 + b0, 16, stride=N), :] = block[
                    b1 * 16 : b1 * 16 + 16
                ]


VMEM_LIMIT = 60 * 2**20
WHOLE = pl.BlockSpec((8, 2 * N, 2 * N), lambda i: (0, 0, 0))


def before(state, stacked):
    return pl.pallas_call(
        before_kernel,
        grid=(32,),
        in_specs=[
            pl.BlockSpec((8, N, N), lambda i: (jnp.minimum(i, 15), 0, 0)),
            WHOLE,
        ],
        out_specs=pl.BlockSpec(
            (8, 1, 8, 16, N), lambda i: (0, jnp.maximum(i - 16, 0), 0, 0, 0)
        ),
        out_shape=jax.ShapeDtypeStruct((8, 16, 8, 16, N), F32),
        scratch_shapes=[pltpu.VMEM((N * N, N), F32)],
        compiler_params=pltpu.CompilerParams(vmem_limit_bytes=VMEM_LIMIT),
        name="before",
    )(state, stacked)


def between(state, stacked):
    return pl.pallas_call(
        between_kernel,
        grid=(24,),
        in_specs=[
            pl.BlockSpec(
                (8, 1, 8, 16, N), lambda i: (0, jnp.minimum(i, 15), 0, 0, 0)
            ),
            WHOLE,
        ],
        out_specs=pl.BlockSpec(
            (1, 16, 8, 16, N), lambda i: (jnp.maximum(i - 16, 0), 0, 0, 0, 0)
        ),
        out_shape=jax.ShapeDtypeStruct((8, 16, 8, 16, N), F32),
        scratch_shapes=[
            pltpu.VMEM((8, 8, 16, N), F32),
            pltpu.VMEM((8, 16, 8, 16, N), F32),
        ],
        compiler_params=pltpu.CompilerParams(vmem_limit_bytes=VMEM_LIMIT),
        name="between",
    )(state, stacked)


def after(state, stacked):
    return pl.pallas_call(
        after_kernel,
        grid=(32,),
        in_specs=[
            pl.BlockSpec(
                (1, 16, 8, 16, N), lambda i: (jnp.minimum(i, 7), 0, 0, 0, 0)
            ),
            WHOLE,
        ],
        out_specs=pl.BlockSpec(
            (16 * N, N), lambda i: (jnp.maximum(i - 24, 0), 0)
        ),
        out_shape=jax.ShapeDtypeStruct((N * N, N), F32),
        scratch_shapes=[
            pltpu.VMEM((16, 16, 8, N), F32),
            pltpu.VMEM((N * N, N), F32),
            pltpu.VMEM((8, 16, 8, 16, N), F32),
        ],
        compiler_params=pltpu.CompilerParams(vmem_limit_bytes=VMEM_LIMIT),
        name="after",
    )(state, stacked)


def exchange(state):
    sent = state.reshape(N, N, N)
    return lax.all_to_all(sent, ("qa", "qb"), 0, 0, tiled=True).reshape(state.shape)


def on_device(amplitudes, gates, qubit_order):
    stacked = stack_gates(gates, qubit_order)
    state = before(amplitudes.reshape(N, N, N), stacked)
    state = between(exchange(state), stacked)
    state = after(exchange(state), stacked)
    return state.reshape(amplitudes.shape)


def solution(mesh):
    return jax.shard_map(
        on_device,
        mesh=mesh,
        in_specs=(P("qa", "qb", None, None, None), P(), P()),
        out_specs=P("qa", "qb", None, None, None),
        check_vma=False,
    )
```

```python
import jax
import jax.numpy as jnp
from jax import lax
from jax.experimental import pallas as pl
from jax.experimental.pallas import tpu as pltpu
from jax.sharding import PartitionSpec as P

N = 128
BF = jnp.bfloat16
F32 = jnp.float32
F0, M0, B0, T0, F1, M1, B1, T1 = range(8)


def split(value, axis):
    high = value.astype(BF)
    low = (value - high.astype(F32)).astype(BF)
    return jnp.concatenate([high, low], axis=axis)


def turn(index, low_bits):
    return ((index & (2**low_bits - 1)) << (7 - low_bits)) | (index >> low_bits)


ROWS = {F1: 4, B1: 4, B0: 3}
COLUMNS = {F1: 4, B1: 4}


def gates_kernel(order_ref, gates_ref, stacked_ref):
    along = lax.broadcasted_iota(jnp.int32, (N, N), 0)
    across = lax.broadcasted_iota(jnp.int32, (N, N), 1)

    def mapped(index, slot):
        total = jnp.zeros_like(index)
        for k in range(7):
            total = total + (((index >> order_ref[slot, k]) & 1) << k)
        return total

    for slot in range(8):
        rows = turn(along, ROWS[slot]) if slot in ROWS else along
        columns = turn(across, COLUMNS[slot]) if slot in COLUMNS else across
        pick_rows = (mapped(rows, slot) == across).astype(F32).astype(BF)
        pick_columns = (mapped(columns, slot) == along).astype(F32).astype(BF)
        picked = jnp.dot(
            pick_rows, split(gates_ref[slot], 1), preferred_element_type=F32
        ).astype(BF)
        both = jnp.concatenate([picked[:, :N], picked[:, N:]], axis=0)
        effective = jnp.dot(both, pick_columns, preferred_element_type=F32).astype(BF)
        stacked_ref[slot] = jnp.concatenate([effective, effective], axis=1)


def stack_gates(gates, qubit_order):
    return pl.pallas_call(
        gates_kernel,
        out_shape=jax.ShapeDtypeStruct((8, 2 * N, 2 * N), BF),
        in_specs=[
            pl.BlockSpec(memory_space=pltpu.SMEM),
            pl.BlockSpec(memory_space=pltpu.VMEM),
        ],
        out_specs=pl.BlockSpec(memory_space=pltpu.VMEM),
        name="stack_gates",
    )(qubit_order.reshape(8, 7), gates.reshape(8, N, N))


def left(gate, blocks):
    width = len(blocks) * N
    value = jnp.concatenate(blocks, axis=1) if len(blocks) > 1 else blocks[0]
    both = jnp.dot(gate, split(value, 0), preferred_element_type=F32)
    total = both[:N] + both[N:]
    return [total[:, k : k + N] for k in range(0, width, N)]


def left_of_transposed(gate, blocks):
    width = len(blocks) * N
    value = jnp.concatenate(blocks, axis=0)
    both = lax.dot_general(
        gate, split(value, 1), (((1,), (1,)), ((), ())), preferred_element_type=F32
    )
    total = both[:N] + both[N:]
    return [total[:, k : k + N] for k in range(0, width, N)]


GROUP = 2
STEPS = 4


def before_kernel(x_ref, gates_ref, out_ref, held):
    step = pl.program_id(0)

    @pl.when(step < STEPS)
    def _():
        gate = gates_ref[M0]
        part = N // STEPS
        for k in range(0, part, GROUP):
            done = left(gate, [x_ref[k + j] for j in range(GROUP)])
            for j in range(GROUP):
                start = pl.multiple_of((step * part + k + j) * N, N)
                held[pl.ds(start, N), :] = done[j]

    @pl.when(step >= STEPS)
    def _():
        gate = gates_ref[F0]
        part = 16 // STEPS
        for i in range(part):
            b0 = (step - STEPS) * part + i
            for k in range(0, 8, GROUP):
                done = left(
                    gate,
                    [
                        held[pl.ds(b0 + (k + j) * 16, N, stride=N), :]
                        for j in range(GROUP)
                    ],
                )
                for j in range(GROUP):
                    out_ref[:, i, k + j] = done[j].reshape(8, 16, N)


def between_kernel(x_ref, gates_ref, out_ref, turned, held):
    step = pl.program_id(0)

    @pl.when(step < STEPS)
    def _():
        part = 16 // STEPS
        for i in range(part):
            gate = gates_ref[T0]
            for k in range(0, 8, GROUP):
                done = left(
                    gate, [x_ref[:, i, k + j].reshape(N, N) for j in range(GROUP)]
                )
                for j in range(GROUP):
                    turned[:, k + j] = done[j].reshape(8, 16, N)
            gate = gates_ref[F1]
            for k in range(0, 8, GROUP):
                done = left(gate, [turned[k + j].reshape(N, N) for j in range(GROUP)])
                for j in range(GROUP):
                    held[k + j, step * part + i] = done[j].reshape(8, 16, N)

    @pl.when(step >= STEPS)
    def _():
        gate = gates_ref[T1]
        part = 8 // STEPS
        for i in range(part):
            x = (step - STEPS) * part + i
            for b1 in range(8):
                done = left(
                    gate, [held[x, :, b1, k : k + 8].reshape(N, N) for k in (0, 8)]
                )
                for j, k in enumerate((0, 8)):
                    out_ref[i, :, b1, k : k + 8] = done[j].reshape(16, 8, N)


def after_kernel(x_ref, gates_ref, out_ref, turned, held, ready):
    step = pl.program_id(0)

    @pl.when(step < STEPS)
    def _():
        part = 8 // STEPS
        for i in range(part):
            gate = gates_ref[B0]
            for k in range(0, 16, GROUP):
                done = left_of_transposed(
                    gate, [x_ref[i, k + j].reshape(N, N) for j in range(GROUP)]
                )
                for j in range(GROUP):
                    turned[:, k + j] = done[j].reshape(16, 8, N)
            gate = gates_ref[M1]
            for k in range(0, 16, GROUP):
                done = left(gate, [turned[k + j].reshape(N, N) for j in range(GROUP)])
                for j in range(GROUP):
                    start = pl.multiple_of(
                        ((step * part + i) * 16 + k + j) * N, N
                    )
                    held[pl.ds(start, N), :] = done[j]

    @pl.when((step >= STEPS) & (step < 2 * STEPS))
    def _():
        gate = gates_ref[B1]
        part = 16 // STEPS
        for i in range(part):
            b0 = (step - STEPS) * part + i
            for k in range(0, 8, GROUP):
                done = left(
                    gate,
                    [
                        held[pl.ds(b0 * 8 + k + j, N, stride=N), :]
                        for j in range(GROUP)
                    ],
                )
                for j in range(GROUP):
                    ready[:, b0, k + j] = done[j].reshape(8, 16, N)

    @pl.when(step >= 2 * STEPS)
    def _():
        part = 8 // STEPS
        for i in range(part):
            a1 = (step - 2 * STEPS) * part + i
            for b0 in range(16):
                block = ready[a1, b0].reshape(N, N).T
                for b1 in range(8):
                    start = i * 16 * N + b1 * 16 + b0
                    out_ref[pl.ds(start, 16, stride=N), :] = block[
                        b1 * 16 : b1 * 16 + 16
                    ]


VMEM_LIMIT = 60 * 2**20
WHOLE = pl.BlockSpec((8, 2 * N, 2 * N), lambda i: (0, 0, 0))


def first(i):
    return jnp.minimum(i, STEPS - 1)


def last(i, earlier):
    return jnp.maximum(i - earlier * STEPS, 0)


def before(state, stacked):
    return pl.pallas_call(
        before_kernel,
        grid=(2 * STEPS,),
        in_specs=[
            pl.BlockSpec((N // STEPS, N, N), lambda i: (first(i), 0, 0)),
            WHOLE,
        ],
        out_specs=pl.BlockSpec(
            (8, 16 // STEPS, 8, 16, N), lambda i: (0, last(i, 1), 0, 0, 0)
        ),
        out_shape=jax.ShapeDtypeStruct((8, 16, 8, 16, N), F32),
        scratch_shapes=[pltpu.VMEM((N * N, N), F32)],
        compiler_params=pltpu.CompilerParams(vmem_limit_bytes=VMEM_LIMIT),
        name="before",
    )(state, stacked)


def between(state, stacked):
    return pl.pallas_call(
        between_kernel,
        grid=(2 * STEPS,),
        in_specs=[
            pl.BlockSpec((8, 16 // STEPS, 8, 16, N), lambda i: (0, first(i), 0, 0, 0)),
            WHOLE,
        ],
        out_specs=pl.BlockSpec(
            (8 // STEPS, 16, 8, 16, N), lambda i: (last(i, 1), 0, 0, 0, 0)
        ),
        out_shape=jax.ShapeDtypeStruct((8, 16, 8, 16, N), F32),
        scratch_shapes=[
            pltpu.VMEM((8, 8, 16, N), F32),
            pltpu.VMEM((8, 16, 8, 16, N), F32),
        ],
        compiler_params=pltpu.CompilerParams(vmem_limit_bytes=VMEM_LIMIT),
        name="between",
    )(state, stacked)


def after(state, stacked):
    return pl.pallas_call(
        after_kernel,
        grid=(3 * STEPS,),
        in_specs=[
            pl.BlockSpec((8 // STEPS, 16, 8, 16, N), lambda i: (first(i), 0, 0, 0, 0)),
            WHOLE,
        ],
        out_specs=pl.BlockSpec((16 // STEPS * 8 * N, N), lambda i: (last(i, 2), 0)),
        out_shape=jax.ShapeDtypeStruct((N * N, N), F32),
        scratch_shapes=[
            pltpu.VMEM((16, 16, 8, N), F32),
            pltpu.VMEM((N * N, N), F32),
            pltpu.VMEM((8, 16, 8, 16, N), F32),
        ],
        compiler_params=pltpu.CompilerParams(vmem_limit_bytes=VMEM_LIMIT),
        name="after",
    )(state, stacked)


def exchange(state):
    sent = state.reshape(N, N, N)
    return lax.all_to_all(sent, ("qa", "qb"), 0, 0, tiled=True).reshape(state.shape)


def on_device(amplitudes, gates, qubit_order):
    stacked = stack_gates(gates, qubit_order)
    state = before(amplitudes.reshape(N, N, N), stacked)
    state = between(exchange(state), stacked)
    state = after(exchange(state), stacked)
    return state.reshape(amplitudes.shape)


def solution(mesh):
    return jax.shard_map(
        on_device,
        mesh=mesh,
        in_specs=(P("qa", "qb", None, None, None), P(), P()),
        out_specs=P("qa", "qb", None, None, None),
        check_vma=False,
    )
```

```python
import jax
import jax.numpy as jnp
from jax import lax
from jax.experimental import pallas as pl
from jax.experimental.pallas import tpu as pltpu
from jax.sharding import PartitionSpec as P

N = 128
BF = jnp.bfloat16
F32 = jnp.float32
F0, M0, B0, T0, F1, M1, B1, T1 = range(8)
BEFORE, BETWEEN, AFTER = (M0, F0), (T0, F1, T1), (B0, M1, B1)


def split(value, axis):
    high = value.astype(BF)
    low = (value - high.astype(F32)).astype(BF)
    return jnp.concatenate([high, low], axis=axis)


def turn(index, low_bits):
    return ((index & (2**low_bits - 1)) << (7 - low_bits)) | (index >> low_bits)


ROWS = {F1: 4, B1: 4, B0: 3}
COLUMNS = {F1: 4, B1: 4}


def effective(slot, order_ref, gates_ref):
    along = lax.broadcasted_iota(jnp.int32, (N, N), 0)
    across = lax.broadcasted_iota(jnp.int32, (N, N), 1)

    def mapped(index):
        total = jnp.zeros_like(index)
        for k in range(7):
            total = total + (((index >> order_ref[slot, k]) & 1) << k)
        return total

    rows = turn(along, ROWS[slot]) if slot in ROWS else along
    columns = turn(across, COLUMNS[slot]) if slot in COLUMNS else across
    pick_rows = (mapped(rows) == across).astype(F32).astype(BF)
    pick_columns = (mapped(columns) == along).astype(F32).astype(BF)
    picked = jnp.dot(
        pick_rows, split(gates_ref[slot], 1), preferred_element_type=F32
    ).astype(BF)
    both = jnp.concatenate([picked[:, :N], picked[:, N:]], axis=0)
    parts = jnp.dot(both, pick_columns, preferred_element_type=F32).astype(BF)
    return jnp.concatenate([parts, parts], axis=1)


def left(gate, blocks):
    width = len(blocks) * N
    value = jnp.concatenate(blocks, axis=1) if len(blocks) > 1 else blocks[0]
    both = jnp.dot(gate, split(value, 0), preferred_element_type=F32)
    total = both[:N] + both[N:]
    return [total[:, k : k + N] for k in range(0, width, N)]


def left_of_transposed(gate, blocks):
    width = len(blocks) * N
    value = jnp.concatenate(blocks, axis=0)
    both = lax.dot_general(
        gate, split(value, 1), (((1,), (1,)), ((), ())), preferred_element_type=F32
    )
    total = both[:N] + both[N:]
    return [total[:, k : k + N] for k in range(0, width, N)]


GROUP = 2
STEPS = 4
ROW = N + 1


def before_kernel(
    x_ref, order_ref, gates_ref, out_ref, between_ref, after_ref, arrived, held, done_in
):
    part = N // STEPS

    def copy(i):
        rows = pl.ds(i * part, part)
        return pltpu.make_async_copy(x_ref.at[rows], arrived.at[rows], done_in.at[i])

    for i in range(STEPS):
        copy(i).start()
    for place, slot in enumerate(BETWEEN):
        between_ref[place] = effective(slot, order_ref, gates_ref)
    for place, slot in enumerate(AFTER):
        after_ref[place] = effective(slot, order_ref, gates_ref)

    middle = effective(M0, order_ref, gates_ref)
    front = effective(F0, order_ref, gates_ref)
    for i in range(STEPS):
        copy(i).wait()

        @pl.loop(0, part, step=16 * GROUP)
        def _(start):
            for k in range(0, 16 * GROUP, GROUP):
                a = i * part + start + k
                done = left(middle, [arrived[a + j] for j in range(GROUP)])
                for j in range(GROUP):
                    held[pl.ds((a + j) * ROW, N), :] = done[j]

    @pl.loop(0, 16, unroll=UNROLL)
    def _(b0):
        for k in range(0, 8, GROUP):
            done = left(
                front,
                [
                    held[pl.ds(b0 + (k + j) * 16, N, stride=ROW), :]
                    for j in range(GROUP)
                ],
            )
            for j in range(GROUP):
                out_ref[:, b0, k + j] = done[j].reshape(8, 16, N)


def between_kernel(x_ref, gates_ref, out_ref, turned, held):
    @pl.loop(0, 16, unroll=UNROLL)
    def _(y):
        gate = gates_ref[0]
        for k in range(0, 8, GROUP):
            done = left(gate, [x_ref[:, y, k + j].reshape(N, N) for j in range(GROUP)])
            for j in range(GROUP):
                turned[:, k + j] = done[j].reshape(8, 16, N)
        gate = gates_ref[1]
        for k in range(0, 8, GROUP):
            done = left(gate, [turned[k + j].reshape(N, N) for j in range(GROUP)])
            for j in range(GROUP):
                held[k + j, y] = done[j].reshape(8, 16, N)

    @pl.loop(0, 8, unroll=UNROLL)
    def _(x):
        gate = gates_ref[2]
        for b1 in range(8):
            done = left(
                gate, [held[x, :, b1, k : k + 8].reshape(N, N) for k in (0, 8)]
            )
            for j, k in enumerate((0, 8)):
                out_ref[x, :, b1, k : k + 8] = done[j].reshape(16, 8, N)


def after_kernel(x_ref, gates_ref, out_ref, turned, held, ready):
    step = pl.program_id(0)

    @pl.when(step == 0)
    def _():
        @pl.loop(0, 8, unroll=UNROLL)
        def _(a1):
            gate = gates_ref[0]
            for k in range(0, 16, GROUP):
                done = left_of_transposed(
                    gate, [x_ref[a1, k + j].reshape(N, N) for j in range(GROUP)]
                )
                for j in range(GROUP):
                    turned[:, k + j] = done[j].reshape(16, 8, N)
            gate = gates_ref[1]
            for k in range(0, 16, GROUP):
                done = left(gate, [turned[k + j].reshape(N, N) for j in range(GROUP)])
                for j in range(GROUP):
                    held[pl.ds((a1 * 16 + k + j) * ROW, N), :] = done[j]

        @pl.loop(0, 16, unroll=UNROLL)
        def _(b0):
            gate = gates_ref[2]
            for k in range(0, 8, GROUP):
                done = left(
                    gate,
                    [
                        held[pl.ds(b0 * 8 + k + j, N, stride=ROW), :]
                        for j in range(GROUP)
                    ],
                )
                for j in range(GROUP):
                    ready[:, b0, k + j] = done[j].reshape(8, 16, N)

    part = 8 // STEPS
    for i in range(part):
        for b0 in range(16):
            block = ready[step * part + i, b0].reshape(N, N).T
            for b1 in range(8):
                start = i * 16 * N + b1 * 16 + b0
                out_ref[pl.ds(start, 16, stride=N), :] = block[b1 * 16 : b1 * 16 + 16]


UNROLL = 8
IN_VMEM = pl.BlockSpec(memory_space=pltpu.VMEM)


def limit(mebibytes):
    return pltpu.CompilerParams(vmem_limit_bytes=mebibytes * 2**20)


def cost(gates):
    return pl.CostEstimate(
        flops=gates * 8 * N**4, bytes_accessed=2**24, transcendentals=0
    )


def before(state, gates, qubit_order):
    return pl.pallas_call(
        before_kernel,
        in_specs=[
            pl.BlockSpec(memory_space=pltpu.HBM),
            pl.BlockSpec(memory_space=pltpu.SMEM),
            IN_VMEM,
        ],
        out_specs=[IN_VMEM] * 3,
        out_shape=[
            pltpu.VMEM((8, 16, 8, 16, N), F32),
            pltpu.VMEM((len(BETWEEN), 2 * N, 2 * N), BF),
            pltpu.VMEM((len(AFTER), 2 * N, 2 * N), BF),
        ],
        scratch_shapes=[
            pltpu.VMEM((N, N, N), F32),
            pltpu.VMEM((N * ROW, N), F32),
            pltpu.SemaphoreType.DMA((STEPS,)),
        ],
        compiler_params=limit(24),
        cost_estimate=cost(2),
        name="before",
    )(
        pltpu.with_memory_space_constraint(state, pltpu.HBM),
        qubit_order.reshape(8, 7),
        gates.reshape(8, N, N),
    )


def between(state, stacked):
    return pl.pallas_call(
        between_kernel,
        in_specs=[IN_VMEM, IN_VMEM],
        out_specs=IN_VMEM,
        out_shape=pltpu.VMEM((8, 16, 8, 16, N), F32),
        scratch_shapes=[
            pltpu.VMEM((8, 8, 16, N), F32),
            pltpu.VMEM((8, 16, 8, 16, N), F32),
        ],
        compiler_params=limit(24),
        cost_estimate=cost(3),
        name="between",
    )(
        pltpu.with_memory_space_constraint(state, pltpu.VMEM),
        pltpu.with_memory_space_constraint(stacked, pltpu.VMEM),
    )


def after(state, stacked):
    return pl.pallas_call(
        after_kernel,
        grid=(STEPS,),
        in_specs=[IN_VMEM, IN_VMEM],
        out_specs=pl.BlockSpec((N // STEPS * N, N), lambda i: (i, 0)),
        out_shape=jax.ShapeDtypeStruct((N * N, N), F32),
        scratch_shapes=[
            pltpu.VMEM((16, 16, 8, N), F32),
            pltpu.VMEM((N * ROW, N), F32),
            pltpu.VMEM((8, 16, 8, 16, N), F32),
        ],
        compiler_params=limit(32),
        cost_estimate=cost(3),
        name="after",
    )(
        pltpu.with_memory_space_constraint(state, pltpu.VMEM),
        pltpu.with_memory_space_constraint(stacked, pltpu.VMEM),
    )


def exchange(state):
    sent = state.reshape(N, N, N)
    return lax.all_to_all(sent, ("qa", "qb"), 0, 0, tiled=True).reshape(state.shape)


def on_device(amplitudes, gates, qubit_order):
    state, in_between, at_end = before(
        amplitudes.reshape(N, N, N), gates, qubit_order
    )
    state = between(exchange(state), in_between)
    state = after(exchange(state), at_end)
    return state.reshape(amplitudes.shape)


def solution(mesh):
    return jax.shard_map(
        on_device,
        mesh=mesh,
        in_specs=(P("qa", "qb", None, None, None), P(), P()),
        out_specs=P("qa", "qb", None, None, None),
        check_vma=False,
    )
```

```python
import jax
import jax.numpy as jnp
from jax import lax
from jax.experimental import pallas as pl
from jax.experimental.pallas import tpu as pltpu
from jax.sharding import PartitionSpec as P

N = 128
BF = jnp.bfloat16
F32 = jnp.float32
F0, M0, B0, T0, F1, M1, B1, T1 = range(8)
BEFORE, BETWEEN, AFTER = (M0, F0), (T0, F1, T1), (B0, M1, B1)


def split(value, axis):
    high = value.astype(BF)
    low = (value - high.astype(F32)).astype(BF)
    return jnp.concatenate([high, low], axis=axis)


def turn(index, low_bits):
    return ((index & (2**low_bits - 1)) << (7 - low_bits)) | (index >> low_bits)


ROWS = {F1: 4, B1: 4, B0: 3}
COLUMNS = {F1: 4, B1: 4}


def effective(slot, order_ref, gates_ref):
    along = lax.broadcasted_iota(jnp.int32, (N, N), 0)
    across = lax.broadcasted_iota(jnp.int32, (N, N), 1)

    def mapped(index):
        total = jnp.zeros_like(index)
        for k in range(7):
            total = total + (((index >> order_ref[slot, k]) & 1) << k)
        return total

    rows = turn(along, ROWS[slot]) if slot in ROWS else along
    columns = turn(across, COLUMNS[slot]) if slot in COLUMNS else across
    pick_rows = (mapped(rows) == across).astype(F32).astype(BF)
    pick_columns = (mapped(columns) == along).astype(F32).astype(BF)
    picked = jnp.dot(
        pick_rows, split(gates_ref[slot], 1), preferred_element_type=F32
    ).astype(BF)
    both = jnp.concatenate([picked[:, :N], picked[:, N:]], axis=0)
    parts = jnp.dot(both, pick_columns, preferred_element_type=F32).astype(BF)
    return jnp.concatenate([parts, parts], axis=1)


def left(gate, blocks):
    width = len(blocks) * N
    value = jnp.concatenate(blocks, axis=1) if len(blocks) > 1 else blocks[0]
    both = jnp.dot(gate, split(value, 0), preferred_element_type=F32)
    total = both[:N] + both[N:]
    return [total[:, k : k + N] for k in range(0, width, N)]


def left_of_transposed(gate, blocks):
    width = len(blocks) * N
    value = jnp.concatenate(blocks, axis=0)
    both = lax.dot_general(
        gate, split(value, 1), (((1,), (1,)), ((), ())), preferred_element_type=F32
    )
    total = both[:N] + both[N:]
    return [total[:, k : k + N] for k in range(0, width, N)]


GROUP = 2
STEPS = 4
PIECES = 8
ROW = N + 1
LINE = N + 8


def before_kernel(
    x_ref,
    order_hbm,
    gates_hbm,
    out_ref,
    between_ref,
    after_ref,
    order_ref,
    gates_ref,
    arrived,
    held,
    done_in,
):
    part = N // STEPS

    def copy(i):
        rows = pl.ds(i * part, part)
        return pltpu.make_async_copy(x_ref.at[rows], arrived.at[rows], done_in.at[i])

    small = [
        pltpu.make_async_copy(order_hbm, order_ref, done_in.at[STEPS]),
        pltpu.make_async_copy(gates_hbm, gates_ref, done_in.at[STEPS + 1]),
    ]
    for one in small:
        one.start()
    for i in range(STEPS):
        copy(i).start()
    for one in small:
        one.wait()
    for place, slot in enumerate(BETWEEN):
        between_ref[place] = effective(slot, order_ref, gates_ref)
    for place, slot in enumerate(AFTER):
        after_ref[place] = effective(slot, order_ref, gates_ref)

    middle = effective(M0, order_ref, gates_ref)
    front = effective(F0, order_ref, gates_ref)
    for i in range(STEPS):
        copy(i).wait()

        @pl.loop(0, part, step=16 * GROUP)
        def _(start):
            for k in range(0, 16 * GROUP, GROUP):
                a = i * part + start + k
                done = left(middle, [arrived[a + j] for j in range(GROUP)])
                for j in range(GROUP):
                    held[pl.ds((a + j) * ROW, N), :] = done[j]

    @pl.loop(0, 16, unroll=UNROLL)
    def _(b0):
        for k in range(0, 8, GROUP):
            done = left(
                front,
                [
                    held[pl.ds(b0 + (k + j) * 16, N, stride=ROW), :]
                    for j in range(GROUP)
                ],
            )
            for j in range(GROUP):
                out_ref[:, b0, k + j] = done[j].reshape(8, 16, N)


def between_kernel(x_ref, gates_ref, out_ref, turned, held):
    @pl.loop(0, 16, unroll=UNROLL)
    def _(y):
        gate = gates_ref[0]
        for k in range(0, 8, GROUP):
            done = left(gate, [x_ref[:, y, k + j].reshape(N, N) for j in range(GROUP)])
            for j in range(GROUP):
                turned[:, k + j] = done[j].reshape(8, 16, N)
        gate = gates_ref[1]
        for k in range(0, 8, GROUP):
            done = left(gate, [turned[k + j].reshape(N, N) for j in range(GROUP)])
            for j in range(GROUP):
                held[k + j, y] = done[j].reshape(8, 16, N)

    @pl.loop(0, 8, unroll=UNROLL)
    def _(x):
        gate = gates_ref[2]
        for b1 in range(8):
            done = left(
                gate, [held[x, :, b1, k : k + 8].reshape(N, N) for k in (0, 8)]
            )
            for j, k in enumerate((0, 8)):
                out_ref[x, :, b1, k : k + 8] = done[j].reshape(16, 8, N)


def after_kernel(x_ref, gates_ref, out_ref, turned, held, ready, lines, done_out):
    @pl.loop(0, 8, unroll=UNROLL)
    def _(a1):
        gate = gates_ref[0]
        for k in range(0, 16, GROUP):
            done = left_of_transposed(
                gate, [x_ref[a1, k + j].reshape(N, N) for j in range(GROUP)]
            )
            for j in range(GROUP):
                turned[:, k + j] = done[j].reshape(16, 8, N)
        gate = gates_ref[1]
        for k in range(0, 16, GROUP):
            done = left(gate, [turned[k + j].reshape(N, N) for j in range(GROUP)])
            for j in range(GROUP):
                held[pl.ds((a1 * 16 + k + j) * ROW, N), :] = done[j]

    @pl.loop(0, 16, unroll=UNROLL)
    def _(b0):
        gate = gates_ref[2]
        for k in range(0, 8, GROUP):
            done = left(
                gate,
                [
                    held[pl.ds(b0 * 8 + k + j, N, stride=ROW), :]
                    for j in range(GROUP)
                ],
            )
            for j in range(GROUP):
                ready[:, b0, k + j] = done[j].reshape(8, 16, N)

    def copy(i):
        part = N // PIECES
        return pltpu.make_async_copy(
            lines.reshape(N, LINE, N).at[pl.ds(i * part, part), pl.ds(0, N)],
            out_ref.at[pl.ds(i * part, part)],
            done_out.at[i],
        )

    part = 8 // PIECES
    for i in range(PIECES):
        for a1 in range(i * part, i * part + part):
            for b0 in range(16):
                block = ready[a1, b0].reshape(N, N).T
                for b1 in range(8):
                    start = a1 * 16 * LINE + b1 * 16 + b0
                    lines[pl.ds(start, 16, stride=LINE), :] = block[
                        b1 * 16 : b1 * 16 + 16
                    ]
        copy(i).start()
    for i in range(PIECES):
        copy(i).wait()


UNROLL = 8
IN_VMEM = pl.BlockSpec(memory_space=pltpu.VMEM)


def limit(mebibytes):
    return pltpu.CompilerParams(vmem_limit_bytes=mebibytes * 2**20)


def cost(gates):
    return pl.CostEstimate(
        flops=gates * 8 * N**4, bytes_accessed=2**24, transcendentals=0
    )


def before(state, gates, qubit_order):
    return pl.pallas_call(
        before_kernel,
        in_specs=[pl.BlockSpec(memory_space=pltpu.HBM)] * 3,
        out_specs=[IN_VMEM] * 3,
        out_shape=[
            pltpu.VMEM((8, 16, 8, 16, N), F32),
            pltpu.VMEM((len(BETWEEN), 2 * N, 2 * N), BF),
            pltpu.VMEM((len(AFTER), 2 * N, 2 * N), BF),
        ],
        scratch_shapes=[
            pltpu.SMEM((8, 7), jnp.int32),
            pltpu.VMEM((8, N, N), F32),
            pltpu.VMEM((N, N, N), F32),
            pltpu.VMEM((N * ROW, N), F32),
            pltpu.SemaphoreType.DMA((STEPS + 2,)),
        ],
        compiler_params=limit(24),
        cost_estimate=cost(2),
        name="before",
    )(
        pltpu.with_memory_space_constraint(state, pltpu.HBM),
        pltpu.with_memory_space_constraint(qubit_order.reshape(8, 7), pltpu.HBM),
        pltpu.with_memory_space_constraint(gates.reshape(8, N, N), pltpu.HBM),
    )


def between(state, stacked):
    return pl.pallas_call(
        between_kernel,
        in_specs=[IN_VMEM, IN_VMEM],
        out_specs=IN_VMEM,
        out_shape=pltpu.VMEM((8, 16, 8, 16, N), F32),
        scratch_shapes=[
            pltpu.VMEM((8, 8, 16, N), F32),
            pltpu.VMEM((8, 16, 8, 16, N), F32),
        ],
        compiler_params=limit(24),
        cost_estimate=cost(3),
        name="between",
    )(
        pltpu.with_memory_space_constraint(state, pltpu.VMEM),
        pltpu.with_memory_space_constraint(stacked, pltpu.VMEM),
    )


def after(state, stacked):
    return pl.pallas_call(
        after_kernel,
        in_specs=[IN_VMEM, IN_VMEM],
        out_specs=pl.BlockSpec(memory_space=pltpu.HBM),
        out_shape=pltpu.HBM((N, N, N), F32),
        scratch_shapes=[
            pltpu.VMEM((16, 16, 8, N), F32),
            pltpu.VMEM((N * ROW, N), F32),
            pltpu.VMEM((8, 16, 8, 16, N), F32),
            pltpu.VMEM((N * LINE, N), F32),
            pltpu.SemaphoreType.DMA((PIECES,)),
        ],
        compiler_params=limit(36),
        cost_estimate=cost(3),
        name="after",
    )(
        pltpu.with_memory_space_constraint(state, pltpu.VMEM),
        pltpu.with_memory_space_constraint(stacked, pltpu.VMEM),
    )


def exchange(state):
    sent = state.reshape(N, N, N)
    return lax.all_to_all(sent, ("qa", "qb"), 0, 0, tiled=True).reshape(state.shape)


def on_device(amplitudes, gates, qubit_order):
    state, in_between, at_end = before(
        amplitudes.reshape(N, N, N), gates, qubit_order
    )
    state = between(exchange(state), in_between)
    state = after(exchange(state), at_end)
    return state.reshape(amplitudes.shape)


def solution(mesh):
    return jax.shard_map(
        on_device,
        mesh=mesh,
        in_specs=(P("qa", "qb", None, None, None), P(), P()),
        out_specs=P("qa", "qb", None, None, None),
        check_vma=False,
    )
```

```python
import jax
import jax.numpy as jnp
from jax import lax
from jax.experimental import pallas as pl
from jax.experimental.pallas import tpu as pltpu
from jax.sharding import PartitionSpec as P

N = 128
BF = jnp.bfloat16
F32 = jnp.float32
F0, M0, B0, T0, F1, M1, B1, T1 = range(8)
BEFORE, BETWEEN, AFTER = (M0, F0), (T0, F1, T1), (B0, M1, B1)


def split(value, axis):
    high = value.astype(BF)
    low = (value - high.astype(F32)).astype(BF)
    return jnp.concatenate([high, low], axis=axis)


def turn(index, low_bits):
    return ((index & (2**low_bits - 1)) << (7 - low_bits)) | (index >> low_bits)


ROWS = {F1: 4, B1: 4, B0: 3}
COLUMNS = {F1: 4, B1: 4}


def effective(slot, order_ref, gates_ref):
    along = lax.broadcasted_iota(jnp.int32, (N, N), 0)
    across = lax.broadcasted_iota(jnp.int32, (N, N), 1)

    def mapped(index):
        total = jnp.zeros_like(index)
        for k in range(7):
            total = total + (((index >> order_ref[slot, k]) & 1) << k)
        return total

    rows = turn(along, ROWS[slot]) if slot in ROWS else along
    columns = turn(across, COLUMNS[slot]) if slot in COLUMNS else across
    pick_rows = (mapped(rows) == across).astype(F32).astype(BF)
    pick_columns = (mapped(columns) == along).astype(F32).astype(BF)
    picked = jnp.dot(
        pick_rows, split(gates_ref[slot], 1), preferred_element_type=F32
    ).astype(BF)
    both = jnp.concatenate([picked[:, :N], picked[:, N:]], axis=0)
    parts = jnp.dot(both, pick_columns, preferred_element_type=F32).astype(BF)
    return jnp.concatenate([parts, parts], axis=1)


def left(gate, blocks):
    width = len(blocks) * N
    value = jnp.concatenate(blocks, axis=1) if len(blocks) > 1 else blocks[0]
    parts = split(value, 0)
    total = jnp.dot(gate[:N], parts, preferred_element_type=F32) + jnp.dot(
        gate[N:, :N], parts[:N], preferred_element_type=F32
    )
    return [total[:, k : k + N] for k in range(0, width, N)]


def left_of_transposed(gate, blocks):
    width = len(blocks) * N
    value = jnp.concatenate(blocks, axis=0)
    both = lax.dot_general(
        gate, split(value, 1), (((1,), (1,)), ((), ())), preferred_element_type=F32
    )
    total = both[:N] + both[N:]
    return [total[:, k : k + N] for k in range(0, width, N)]


GROUP = 2
STEPS = 4
PIECES = 8
ROW = N + 1
LINE = N + 8


def before_kernel(
    x_ref,
    order_hbm,
    gates_hbm,
    out_ref,
    between_ref,
    after_ref,
    order_ref,
    gates_ref,
    arrived,
    held,
    done_in,
):
    part = N // STEPS

    def copy(i):
        rows = pl.ds(i * part, part)
        return pltpu.make_async_copy(x_ref.at[rows], arrived.at[rows], done_in.at[i])

    small = [
        pltpu.make_async_copy(order_hbm, order_ref, done_in.at[STEPS]),
        pltpu.make_async_copy(gates_hbm, gates_ref, done_in.at[STEPS + 1]),
    ]
    for one in small:
        one.start()
    for i in range(STEPS):
        copy(i).start()
    for one in small:
        one.wait()
    for place, slot in enumerate(BETWEEN):
        between_ref[place] = effective(slot, order_ref, gates_ref)
    for place, slot in enumerate(AFTER):
        after_ref[place] = effective(slot, order_ref, gates_ref)

    middle = effective(M0, order_ref, gates_ref)
    front = effective(F0, order_ref, gates_ref)
    for i in range(STEPS):
        copy(i).wait()

        @pl.loop(0, part, step=16 * GROUP)
        def _(start):
            for k in range(0, 16 * GROUP, GROUP):
                a = i * part + start + k
                done = left(middle, [arrived[a + j] for j in range(GROUP)])
                for j in range(GROUP):
                    held[pl.ds((a + j) * ROW, N), :] = done[j]

    @pl.loop(0, 16, unroll=UNROLL)
    def _(b0):
        for k in range(0, 8, GROUP):
            done = left(
                front,
                [
                    held[pl.ds(b0 + (k + j) * 16, N, stride=ROW), :]
                    for j in range(GROUP)
                ],
            )
            for j in range(GROUP):
                out_ref[:, b0, k + j] = done[j].reshape(8, 16, N)


def between_kernel(x_ref, gates_ref, out_ref, turned, held):
    @pl.loop(0, 16, unroll=UNROLL)
    def _(y):
        gate = gates_ref[0]
        for k in range(0, 8, GROUP):
            done = left(gate, [x_ref[:, y, k + j].reshape(N, N) for j in range(GROUP)])
            for j in range(GROUP):
                turned[:, k + j] = done[j].reshape(8, 16, N)
        gate = gates_ref[1]
        for k in range(0, 8, GROUP):
            done = left(gate, [turned[k + j].reshape(N, N) for j in range(GROUP)])
            for j in range(GROUP):
                held[k + j, y] = done[j].reshape(8, 16, N)

    @pl.loop(0, 8, unroll=UNROLL)
    def _(x):
        gate = gates_ref[2]
        for b1 in range(8):
            done = left(
                gate, [held[x, :, b1, k : k + 8].reshape(N, N) for k in (0, 8)]
            )
            for j, k in enumerate((0, 8)):
                out_ref[x, :, b1, k : k + 8] = done[j].reshape(16, 8, N)


def after_kernel(x_ref, gates_ref, out_ref, turned, held, ready, lines, done_out):
    @pl.loop(0, 8, unroll=UNROLL)
    def _(a1):
        gate = gates_ref[0]
        for k in range(0, 16, GROUP):
            done = left_of_transposed(
                gate, [x_ref[a1, k + j].reshape(N, N) for j in range(GROUP)]
            )
            for j in range(GROUP):
                turned[:, k + j] = done[j].reshape(16, 8, N)
        gate = gates_ref[1]
        for k in range(0, 16, GROUP):
            done = left(gate, [turned[k + j].reshape(N, N) for j in range(GROUP)])
            for j in range(GROUP):
                held[pl.ds((a1 * 16 + k + j) * ROW, N), :] = done[j]

    @pl.loop(0, 16, unroll=UNROLL)
    def _(b0):
        gate = gates_ref[2]
        for k in range(0, 8, GROUP):
            done = left(
                gate,
                [
                    held[pl.ds(b0 * 8 + k + j, N, stride=ROW), :]
                    for j in range(GROUP)
                ],
            )
            for j in range(GROUP):
                ready[:, b0, k + j] = done[j].reshape(8, 16, N)

    def copy(i):
        part = N // PIECES
        return pltpu.make_async_copy(
            lines.reshape(N, LINE, N).at[pl.ds(i * part, part), pl.ds(0, N)],
            out_ref.at[pl.ds(i * part, part)],
            done_out.at[i],
        )

    part = 8 // PIECES
    for i in range(PIECES):
        for a1 in range(i * part, i * part + part):
            for b0 in range(16):
                block = ready[a1, b0].reshape(N, N).T
                for b1 in range(8):
                    start = a1 * 16 * LINE + b1 * 16 + b0
                    lines[pl.ds(start, 16, stride=LINE), :] = block[
                        b1 * 16 : b1 * 16 + 16
                    ]
        copy(i).start()
    for i in range(PIECES):
        copy(i).wait()


UNROLL = 8
IN_VMEM = pl.BlockSpec(memory_space=pltpu.VMEM)


def limit(mebibytes):
    return pltpu.CompilerParams(vmem_limit_bytes=mebibytes * 2**20)


def cost(gates):
    return pl.CostEstimate(
        flops=gates * 8 * N**4, bytes_accessed=2**24, transcendentals=0
    )


def before(state, gates, qubit_order):
    return pl.pallas_call(
        before_kernel,
        in_specs=[pl.BlockSpec(memory_space=pltpu.HBM)] * 3,
        out_specs=[IN_VMEM] * 3,
        out_shape=[
            pltpu.VMEM((8, 16, 8, 16, N), F32),
            pltpu.VMEM((len(BETWEEN), 2 * N, 2 * N), BF),
            pltpu.VMEM((len(AFTER), 2 * N, 2 * N), BF),
        ],
        scratch_shapes=[
            pltpu.SMEM((8, 7), jnp.int32),
            pltpu.VMEM((8, N, N), F32),
            pltpu.VMEM((N, N, N), F32),
            pltpu.VMEM((N * ROW, N), F32),
            pltpu.SemaphoreType.DMA((STEPS + 2,)),
        ],
        compiler_params=limit(24),
        cost_estimate=cost(2),
        name="before",
    )(
        pltpu.with_memory_space_constraint(state, pltpu.HBM),
        pltpu.with_memory_space_constraint(qubit_order.reshape(8, 7), pltpu.HBM),
        pltpu.with_memory_space_constraint(gates.reshape(8, N, N), pltpu.HBM),
    )


def between(state, stacked):
    return pl.pallas_call(
        between_kernel,
        in_specs=[IN_VMEM, IN_VMEM],
        out_specs=IN_VMEM,
        out_shape=pltpu.VMEM((8, 16, 8, 16, N), F32),
        scratch_shapes=[
            pltpu.VMEM((8, 8, 16, N), F32),
            pltpu.VMEM((8, 16, 8, 16, N), F32),
        ],
        compiler_params=limit(24),
        cost_estimate=cost(3),
        name="between",
    )(
        pltpu.with_memory_space_constraint(state, pltpu.VMEM),
        pltpu.with_memory_space_constraint(stacked, pltpu.VMEM),
    )


def after(state, stacked):
    return pl.pallas_call(
        after_kernel,
        in_specs=[IN_VMEM, IN_VMEM],
        out_specs=pl.BlockSpec(memory_space=pltpu.HBM),
        out_shape=pltpu.HBM((N, N, N), F32),
        scratch_shapes=[
            pltpu.VMEM((16, 16, 8, N), F32),
            pltpu.VMEM((N * ROW, N), F32),
            pltpu.VMEM((8, 16, 8, 16, N), F32),
            pltpu.VMEM((N * LINE, N), F32),
            pltpu.SemaphoreType.DMA((PIECES,)),
        ],
        compiler_params=limit(36),
        cost_estimate=cost(3),
        name="after",
    )(
        pltpu.with_memory_space_constraint(state, pltpu.VMEM),
        pltpu.with_memory_space_constraint(stacked, pltpu.VMEM),
    )


def exchange(state):
    sent = state.reshape(N, N, N)
    return lax.all_to_all(sent, ("qa", "qb"), 0, 0, tiled=True).reshape(state.shape)


def on_device(amplitudes, gates, qubit_order):
    state, in_between, at_end = before(
        amplitudes.reshape(N, N, N), gates, qubit_order
    )
    state = between(exchange(state), in_between)
    state = after(exchange(state), at_end)
    return state.reshape(amplitudes.shape)


def solution(mesh):
    return jax.shard_map(
        on_device,
        mesh=mesh,
        in_specs=(P("qa", "qb", None, None, None), P(), P()),
        out_specs=P("qa", "qb", None, None, None),
        check_vma=False,
    )
```
